256 devices in a mesh: ctx: 64 (over y, x_hi, z), head: 4 (over x_lo, core).
Axes of the slice: x: 4 (x_hi: 2, x_lo: 2; x = x_hi * 2 + x_lo), y: 4, z: 8, core: 2. Of those that a mesh axis runs over, the one named last changes fastest.
Arguments:
- query_input: bfloat16 [16384, 4096], P('ctx', 'head'), may hold values from -6 to 6
- key_entries_raw: bfloat16 [16384, 1024], P('ctx', 'head'), may hold values from -6 to 6
- value_entries_raw: bfloat16 [16384, 1024], P('ctx', 'head'), may hold values from -6 to 6
- out_grad: bfloat16 [16384, 4096], P('ctx', 'head'), may hold values from -6 to 6
- attn_out: bfloat16 [16384, 4096], P('ctx', 'head'), may hold values from -3 to 3
- log_sum_exp: float32 [32, 16384], P('head', 'ctx'), may hold values from 4 to 6
- positions: int32 [3, 16384], P(None, ('ctx', 'head')), may hold values from 0 to 4095
- span_map: int32 [64], replicated, may hold values from 0 to 63, each once
Outputs:
- query_grad: bfloat16 [16384, 4096], P('ctx', 'head')
- key_gradient_raw: bfloat16 [16384, 1024], P('ctx', 'head')
- value_gradient_rows: bfloat16 [16384, 1024], P('ctx', 'head')
The draws below stay inside these ranges and needn't reach their ends.
Inputs may be any that keep to these rules, and one draw needn't show every extreme that they name: Block b of 256 rows holds span span_map[b] of the sequence in its first 128 rows and span 2 * 64 - 1 - span_map[b] in its last 128 rows; each number appears once.
All inputs are finite; a program needn't handle non-finite values.
Results may differ from the reference program's by a relative error of at most 0.019.
The reference program's roundings to bfloat16 on the way (of `rounded_weights` and `rounded_grad`) count: a program that leaves them out, or rounds other values in their place, can miss the bound.
Values may be sent and summed in bfloat16 or wider, within the bound.
A program may use at most 64 MiB of HBM per device.

```python
import math
import jax
import jax.numpy as jnp
from jax import lax

HQ = 32
KEY_VALUE_HEADS = 8
HEAD_ENTRIES = 128
WIN = 4
TOKENS_PER_PART = 256
SEQUENCE_TOKENS = 16384
N_CTX = 64


def set_ends(entries, stream_key, least, high):
    shape = entries.shape
    index_at = [jax.random.randint(jax.random.fold_in(stream_key, axis), (), 0, shape[axis]) for axis in range(len(shape))]
    entries = entries.at[tuple(index_at)].set(least)
    longest = shape.index(max(shape))
    index_at[longest] = (index_at[longest] + 1) % shape[longest]
    return entries.at[tuple(index_at)].set(high)


def block_scale(rng, dims, cuts, low, top_value):
    level, own = 1.0, jax.random.fold_in(rng, 6)
    for position, blocks in cuts:
        heights = jnp.exp(jax.random.uniform(jax.random.fold_in(own, position), (blocks,), jnp.float32, low / len(cuts), top_value / len(cuts)))
        level = level * jnp.repeat(heights, dims[position] // blocks).reshape([-1 if axis == position else 1 for axis in range(len(dims))])
    return level


def noise(rng, shape, spread, bound, shards=(), held_as=jnp.bfloat16):
    array = jax.random.normal(rng, shape, jnp.float32) * spread
    if len(shards) > 0:
        array = block_scale(rng, shape, shards, -0.22, 0.18) * array
    return jnp.clip(array, min=-bound, max=bound).astype(held_as)


def setup_inputs(seed: int = 0) -> dict:
    arg_keys = jax.random.split(jax.random.key(seed), 9)
    return {
        "query_input": noise(arg_keys[0], (SEQUENCE_TOKENS, HQ * HEAD_ENTRIES), 1.0, 6.0, ((0, 64), (1, 4))),
        "key_entries_raw": noise(arg_keys[1], (SEQUENCE_TOKENS, KEY_VALUE_HEADS * HEAD_ENTRIES), 1.0, 6.0, ((0, 64), (1, 4))),
        "value_entries_raw": noise(arg_keys[2], (SEQUENCE_TOKENS, KEY_VALUE_HEADS * HEAD_ENTRIES), 1.0, 6.0, ((0, 64), (1, 4))),
        "out_grad": noise(arg_keys[3], (SEQUENCE_TOKENS, HQ * HEAD_ENTRIES), 1.0, 6.0, ((0, 64), (1, 4))),
        "attn_out": noise(arg_keys[4], (SEQUENCE_TOKENS, HQ * HEAD_ENTRIES), 0.5, 3.0, ((0, 64), (1, 4))),
        "log_sum_exp": jnp.clip(4.0 + 2.0 * jax.random.uniform(arg_keys[5], (HQ, SEQUENCE_TOKENS), jnp.float32) ** block_scale(arg_keys[5], (HQ, SEQUENCE_TOKENS), ((0, 4), (1, 64)), -0.2, 0.2), 4.0, 6.0),
        "positions": set_ends(jax.random.randint(arg_keys[6], (3, SEQUENCE_TOKENS), 0, 4096), jax.random.fold_in(arg_keys[6], 1), 0, 4095).astype(jnp.int32),
        "span_map": jax.random.permutation(arg_keys[7], N_CTX).astype(jnp.int32),
    }


ROPE_BASE = 1000000.0
YARN_FACTOR = 4.0
YARN_INITIAL = 32768.0
BETA_FAST = 32.0
BETA_SLOW = 1.0
YARN_MSCALE = 1.0 + 0.1 * math.log(4.0)

def rope_tables(positions, head_width):
    half_width = head_width // 2
    pair_index = jnp.arange(half_width, dtype=jnp.float32)
    inverse = jnp.exp(-2.0 * pair_index / head_width * math.log(ROPE_BASE))
    ratio_value = YARN_INITIAL * inverse / (2.0 * math.pi)
    ramp_value = jnp.clip((ratio_value - BETA_SLOW) / (BETA_FAST - BETA_SLOW), 0.0, 1.0)
    frequency = inverse * ((1.0 - ramp_value) / YARN_FACTOR + ramp_value)
    first_cut = head_width // 8
    second_cut = first_cut + 3 * head_width // 16
    spot_values = positions.astype(jnp.float32)
    chosen = jnp.where(pair_index < first_cut, spot_values[0][:, None], jnp.where(pair_index < second_cut, spot_values[1][:, None], spot_values[2][:, None]))
    angles = chosen * frequency
    return (jnp.cos(angles) * YARN_MSCALE, jnp.sin(angles) * YARN_MSCALE)

def apply_rotary(block_rows, cosine_lookup, sine_lookup):
    half_width = block_rows.shape[-1] // 2
    widened = block_rows.astype(jnp.float32)
    first_half = widened[..., :half_width]
    second_half = widened[..., half_width:]
    cosine_rows = cosine_lookup[:, None, :]
    sine_rows = sine_lookup[:, None, :]
    return jnp.concatenate([first_half * cosine_rows - second_half * sine_rows, second_half * cosine_rows + first_half * sine_rows], axis=-1)

def reverse_rotary(gradient, cosine_lookup, sine_lookup):
    half_width = gradient.shape[-1] // 2
    first_half = gradient[..., :half_width]
    second_half = gradient[..., half_width:]
    cosine_rows = cosine_lookup[:, None, :]
    sine_rows = sine_lookup[:, None, :]
    return jnp.concatenate([first_half * cosine_rows + second_half * sine_rows, second_half * cosine_rows - first_half * sine_rows], axis=-1)

def block_grads(query_side, key_side, query_order, key_order):
    query_rotated, grad_heads, norm_rows, delta_rows = query_side
    key_turned, value_head_split = key_side
    row_count = query_rotated.shape[0]
    key_heads = key_turned.shape[1]
    head_width = key_turned.shape[2]
    group_size = query_rotated.shape[1] // key_heads
    root_scale = 1.0 / math.sqrt(head_width)
    query_groups = query_rotated.reshape(row_count, key_heads, group_size, head_width).astype(jnp.float32)
    grad_groups = grad_heads.reshape(row_count, key_heads, group_size, head_width).astype(jnp.float32)
    key_wide = key_turned.astype(jnp.float32)
    value_wide = value_head_split.astype(jnp.float32)
    scores = jnp.einsum('qgjd,kgd->gjqk', query_groups, key_wide) * root_scale
    visible = key_order[None, :] <= query_order[:, None]
    norm_table = norm_rows.reshape(key_heads, group_size, row_count)[..., None]
    weights = jnp.where(visible, jnp.exp(scores - norm_table), 0.0)
    rounded_weights = lax.optimization_barrier(weights.astype(jnp.bfloat16)).astype(jnp.float32)
    value_part = jnp.einsum('gjqk,qgjd->kgd', rounded_weights, grad_groups)
    weight_grad = jnp.einsum('qgjd,kgd->gjqk', grad_groups, value_wide)
    score_grad = weights * (weight_grad - delta_rows.reshape(key_heads, group_size, row_count)[..., None])
    rounded_grad = lax.optimization_barrier(score_grad.astype(jnp.bfloat16)).astype(jnp.float32)
    key_part = jnp.einsum('gjqk,qgjd->kgd', rounded_grad, query_groups) * root_scale
    query_part = jnp.einsum('gjqk,kgd->qgjd', rounded_grad, key_wide).reshape(row_count, key_heads * group_size, head_width) * root_scale
    return (query_part, key_part, value_part)

def reference(query_input, key_entries_raw, value_entries_raw, out_grad, attn_out, log_sum_exp, positions, span_map):
    cosine_lookup, sine_lookup = rope_tables(positions, HEAD_ENTRIES)
    query_rotated = apply_rotary(query_input.reshape(SEQUENCE_TOKENS, HQ, HEAD_ENTRIES), cosine_lookup, sine_lookup).astype(jnp.bfloat16)
    key_turned = apply_rotary(key_entries_raw.reshape(SEQUENCE_TOKENS, KEY_VALUE_HEADS, HEAD_ENTRIES), cosine_lookup, sine_lookup).astype(jnp.bfloat16)
    grad_heads = out_grad.reshape(SEQUENCE_TOKENS, HQ, HEAD_ENTRIES)
    value_head_split = value_entries_raw.reshape(SEQUENCE_TOKENS, KEY_VALUE_HEADS, HEAD_ENTRIES)
    delta_rows = lax.optimization_barrier(jnp.sum(grad_heads.astype(jnp.float32) * attn_out.reshape(SEQUENCE_TOKENS, HQ, HEAD_ENTRIES).astype(jnp.float32), axis=2)).T
    span_len = TOKENS_PER_PART // 2
    offsets = jnp.arange(span_len, dtype=jnp.int32)
    early_span = span_map.astype(jnp.int32)
    late_span = 2 * N_CTX - 1 - early_span
    order = jnp.concatenate([early_span[:, None] * span_len + offsets[None, :], late_span[:, None] * span_len + offsets[None, :]], axis=1)
    query_slots = query_rotated.reshape(N_CTX, TOKENS_PER_PART, HQ, HEAD_ENTRIES)
    grad_slots = grad_heads.reshape(N_CTX, TOKENS_PER_PART, HQ, HEAD_ENTRIES)
    key_places = key_turned.reshape(N_CTX, TOKENS_PER_PART, KEY_VALUE_HEADS, HEAD_ENTRIES)
    value_places = value_head_split.reshape(N_CTX, TOKENS_PER_PART, KEY_VALUE_HEADS, HEAD_ENTRIES)
    norm_slots = log_sum_exp.reshape(HQ, N_CTX, TOKENS_PER_PART).transpose(1, 0, 2)
    delta_slots = delta_rows.reshape(HQ, N_CTX, TOKENS_PER_PART).transpose(1, 0, 2)
    query_total = jnp.zeros((N_CTX, TOKENS_PER_PART, HQ, HEAD_ENTRIES), jnp.float32)
    key_overall = jnp.zeros((N_CTX, TOKENS_PER_PART, KEY_VALUE_HEADS, HEAD_ENTRIES), jnp.float32)
    value_overall = jnp.zeros((N_CTX, TOKENS_PER_PART, KEY_VALUE_HEADS, HEAD_ENTRIES), jnp.float32)
    for hop_index in range(WIN):

        def per_slot(slot_index):
            key_slot = ((slot_index + hop_index) % N_CTX).astype(jnp.int32)
            return block_grads((query_slots[slot_index], grad_slots[slot_index], norm_slots[slot_index], delta_slots[slot_index]), (key_places[key_slot], value_places[key_slot]), order[slot_index], order[key_slot])
        query_part, key_part, value_part = lax.map(per_slot, jnp.arange(N_CTX, dtype=jnp.int32))
        query_total = query_total + query_part
        key_overall = key_overall + jnp.roll(key_part, hop_index, axis=0)
        value_overall = value_overall + jnp.roll(value_part, hop_index, axis=0)
    query_grad = reverse_rotary(query_total.reshape(SEQUENCE_TOKENS, HQ, HEAD_ENTRIES), cosine_lookup, sine_lookup).reshape(SEQUENCE_TOKENS, HQ * HEAD_ENTRIES).astype(jnp.bfloat16)
    key_gradient_raw = reverse_rotary(key_overall.reshape(SEQUENCE_TOKENS, KEY_VALUE_HEADS, HEAD_ENTRIES), cosine_lookup, sine_lookup).reshape(SEQUENCE_TOKENS, KEY_VALUE_HEADS * HEAD_ENTRIES).astype(jnp.bfloat16)
    value_gradient_rows = value_overall.reshape(SEQUENCE_TOKENS, KEY_VALUE_HEADS * HEAD_ENTRIES).astype(jnp.bfloat16)
    return (query_grad, key_gradient_raw, value_gradient_rows)
```

```python
import functools
import math

import jax
import jax.numpy as jnp
from jax import lax
from jax.experimental import pallas as pl
from jax.experimental.pallas import tpu as pltpu
from jax.sharding import PartitionSpec as P

WIDTH = 128
HALF = WIDTH // 2
SPAN = 128
WIN = 4
ROPE_BASE = 1000000.0
YARN_FACTOR = 4.0
YARN_INITIAL = 32768.0
BETA_FAST = 32.0
BETA_SLOW = 1.0
YARN_MSCALE = 1.0 + 0.1 * math.log(4.0)
ROOT_SCALE = 1.0 / math.sqrt(WIDTH)
LOG2E = math.log2(math.e)
F32 = jnp.float32
BF16 = jnp.bfloat16
MESH = pl.DeviceIdType.MESH


def half_pi_parts():
    a = math.floor(math.pi / 2 * 2**11) / 2**11
    rest = math.pi / 2 - a
    shift = 11 - math.floor(math.log2(rest))
    b = math.floor(rest * 2.0**shift) / 2.0**shift
    return a, b, rest - b


def cos_sin(angle):
    a, b, c = half_pi_parts()
    turns = jnp.floor(angle * (2.0 / math.pi) + 0.5)
    rest = ((angle - turns * a) - turns * b) - turns * c
    quadrant = turns.astype(jnp.int32) & 3
    square = rest * rest
    sine = rest + rest * square * (
        -1.0 / 6 + square * (1.0 / 120 + square * (-1.0 / 5040 + square * (1.0 / 362880)))
    )
    cosine = 1.0 + square * (
        -0.5
        + square
        * (1.0 / 24 + square * (-1.0 / 720 + square * (1.0 / 40320 - square * (1.0 / 3628800))))
    )
    swap = (quadrant & 1) == 1
    cos_out = jnp.where(swap, sine, cosine)
    sin_out = jnp.where(swap, cosine, sine)
    cos_out = jnp.where((quadrant == 1) | (quadrant == 2), -cos_out, cos_out)
    sin_out = jnp.where(quadrant >= 2, -sin_out, sin_out)
    return cos_out, sin_out


def frequencies(shape):
    pair = lax.broadcasted_iota(jnp.int32, shape, 0).astype(F32)
    inverse = jnp.exp(-2.0 * pair / WIDTH * math.log(ROPE_BASE))
    ratio = YARN_INITIAL * inverse / (2.0 * math.pi)
    ramp = jnp.clip((ratio - BETA_SLOW) / (BETA_FAST - BETA_SLOW), 0.0, 1.0)
    return inverse * ((1.0 - ramp) / YARN_FACTOR + ramp)


def dot(a, b, a_dim, b_dim):
    return lax.dot_general(a, b, (((a_dim,), (b_dim,)), ((), ())), preferred_element_type=F32)


def kernel(
    groups,
    share,
    n_ctx,
    n_head,
    span_ref,
    q_hbm,
    k_hbm,
    v_hbm,
    g_hbm,
    o_hbm,
    lse_hbm,
    pos_hbm,
    dq_hbm,
    dk_hbm,
    dv_hbm,
    q_raw,
    k_raw,
    g_raw,
    o_raw,
    lse_raw,
    pos_all,
    q_s,
    g_s,
    lse_s,
    delta_s,
    tab_t,
    tab_n,
    kbuf,
    vbuf,
    dq_acc,
    dq_out,
    own,
    part,
    ret_send,
    ret_recv,
    dkv_out,
    load_sem,
    store_sem,
    pos_ssem,
    pos_rsem,
    fwd_ssem,
    fwd_rsem,
    ret_ssem,
    ret_rsem,
):
    me = lax.axis_index("ctx")
    my_head = lax.axis_index("head")
    left = lax.rem(me + (n_ctx - 1), n_ctx)
    right = lax.rem(me + 1, n_ctx)
    peers = [lax.rem(my_head + step, n_head) for step in range(1, n_head)]

    loads = {}

    def load(name, index, source, target):
        loads[name] = pltpu.make_async_copy(source, target, load_sem.at[index])
        loads[name].start()

    load("pos", 0, pos_hbm, pos_all.at[my_head])
    for g in range(groups):
        for half in range(2):
            load(
                ("v", g, half),
                1 + 2 * g + half,
                v_hbm.at[half * SPAN : (half + 1) * SPAN, g * WIDTH : (g + 1) * WIDTH],
                vbuf.at[0, g, half],
            )
    base = 1 + 2 * groups
    load("k", base, k_hbm, k_raw)
    load("q", base + 1, q_hbm, q_raw)
    load("g", base + 2, g_hbm, g_raw)
    load("o", base + 3, o_hbm, o_raw)
    load("lse", base + 4, lse_hbm, lse_raw)

    barrier = pltpu.get_barrier_semaphore()
    for ctx in (left, right):
        pl.semaphore_signal(barrier, inc=1, device_id=(ctx, my_head), device_id_type=MESH)
    for peer in peers:
        pl.semaphore_signal(barrier, inc=1, device_id=(me, peer), device_id_type=MESH)
    freq = frequencies((HALF, WIDTH))
    loads["pos"].wait()
    pl.semaphore_wait(barrier, 2 + len(peers))

    pos_copies = []
    for step, peer in enumerate(peers):
        copy = pltpu.make_async_remote_copy(
            src_ref=pos_all.at[my_head],
            dst_ref=pos_all.at[my_head],
            send_sem=pos_ssem.at[step],
            recv_sem=pos_rsem.at[step],
            device_id=(me, peer),
            device_id_type=MESH,
        )
        copy.start()
        pos_copies.append(copy)

    def forward(which, g, hop):
        buf = (vbuf, kbuf)[which]
        return pltpu.make_async_remote_copy(
            src_ref=buf.at[hop - 1, g],
            dst_ref=buf.at[hop, g],
            send_sem=fwd_ssem.at[which, g, hop - 1],
            recv_sem=fwd_rsem.at[which, g, hop - 1],
            device_id=(left, my_head),
            device_id_type=MESH,
        )

    def send_v(g, hop):
        forward(0, g, hop).start()

    def send_k(g, hop):
        forward(1, g, hop).start()

    def got_v(g, hop):
        forward(0, g, hop).wait_recv()

    def got_k(g, hop):
        forward(1, g, hop).wait_recv()

    for g in range(groups):
        for half in range(2):
            loads[("v", g, half)].wait()
        send_v(g, 1)

    for copy in pos_copies:
        copy.wait_recv()
    pieces = [pos_all[h].astype(F32) for h in range(n_head)]
    placed = jnp.concatenate(pieces, axis=1)
    pair = lax.broadcasted_iota(jnp.int32, (HALF, 2 * SPAN), 0)
    chosen = jnp.where(
        pair < WIDTH // 8,
        placed[0:1],
        jnp.where(pair < WIDTH // 8 + 3 * WIDTH // 16, placed[1:2], placed[2:3]),
    )
    cosine, sine = cos_sin(chosen * jnp.concatenate([freq, freq], axis=1))
    cosine = cosine * YARN_MSCALE
    sine = sine * YARN_MSCALE
    tab_t[0] = cosine
    tab_t[1] = sine
    tab_n[0] = jnp.concatenate([cosine, cosine], axis=0).T
    tab_n[1] = jnp.concatenate([-sine, sine], axis=0).T

    def rotated(block, half):
        wide = block.astype(F32)
        rows = slice(half * SPAN, (half + 1) * SPAN)
        return (wide * tab_n[0, rows] + pltpu.roll(wide, HALF, 1) * tab_n[1, rows]).astype(BF16)

    def unrotated(wide, half):
        rows = slice(half * SPAN, (half + 1) * SPAN)
        return wide * tab_n[0, rows] - pltpu.roll(wide, HALF, 1) * tab_n[1, rows]

    loads["k"].wait()
    for g in range(groups):
        for half in range(2):
            kbuf[0, g, half] = rotated(
                k_raw[half * SPAN : (half + 1) * SPAN, g * WIDTH : (g + 1) * WIDTH], half
            )
        if g == 0:
            send_k(0, 1)

    def prepare(g):
        for half in range(2):
            rows = slice(half * SPAN, (half + 1) * SPAN)
            ones = jnp.ones((8, WIDTH), BF16)
            for j in range(share):
                head = g * share + j
                cols = slice(head * WIDTH, (head + 1) * WIDTH)
                stacked = slice(j * SPAN, (j + 1) * SPAN)
                q_s[g, half, stacked] = rotated(q_raw[rows, cols], half)
                grad = g_raw[rows, cols]
                g_s[g, half, stacked] = grad
                product = grad.astype(F32) * o_raw[rows, cols].astype(F32)
                upper = product.astype(BF16)
                lower = (product - upper.astype(F32)).astype(BF16)
                delta = dot(ones, upper, 1, 1) + dot(ones, lower, 1, 1)
                delta_s[g, half, :, stacked] = delta
                lse_s[g, half, :, stacked] = jnp.broadcast_to(
                    lse_raw[head : head + 1, rows] * LOG2E, (8, SPAN)
                )

    step_cols = 2 * SPAN

    def unit(g, q_half, key, value, masked):
        value_sum = key_sum = None
        query_parts = []
        for start in range(0, share * SPAN, step_cols):
            at = slice(start, start + step_cols)
            query = q_s[g, q_half, at]
            grad = g_s[g, q_half, at]
            scores = dot(key, query, 1, 1)
            exponent = scores * (ROOT_SCALE * LOG2E) - lse_s[g, q_half, 0:1, at]
            weights = jnp.exp2(exponent)
            if masked:
                shape = (SPAN, step_cols)
                key_at = lax.broadcasted_iota(jnp.int32, shape, 0)
                query_at = lax.broadcasted_iota(jnp.int32, shape, 1) & (SPAN - 1)
                weights = jnp.where(key_at <= query_at, weights, 0.0)
            weight_grad = dot(value, grad, 1, 1)
            score_grad = weights * (weight_grad - delta_s[g, q_half, 0:1, at])
            rounded_weights = weights.astype(BF16)
            rounded_grad = score_grad.astype(BF16)
            value_part = dot(rounded_weights, grad, 1, 0)
            key_part = dot(rounded_grad, query, 1, 0)
            value_sum = value_part if value_sum is None else value_sum + value_part
            key_sum = key_part if key_sum is None else key_sum + key_part
            query_parts.append(dot(key, rounded_grad, 0, 0))
        return value_sum, key_sum, jnp.concatenate(query_parts, axis=1)

    my_span = span_ref[me]

    def own_block(g):
        k0, k1, v0, v1 = kbuf[0, g, 0], kbuf[0, g, 1], vbuf[0, g, 0], vbuf[0, g, 1]
        dv, dk, dq = unit(g, 0, k0, v0, True)
        dq_acc[g, 0] = dq
        dv_next, dk_next, dq = unit(g, 1, k0, v0, False)
        own[g, 0, 0] = dv + dv_next
        own[g, 1, 0] = dk + dk_next
        dv, dk, dq_next = unit(g, 1, k1, v1, True)
        own[g, 0, 1] = dv
        own[g, 1, 1] = dk
        dq_acc[g, 1] = dq + dq_next

    def other_block(g, hop):
        lower = span_ref[lax.rem(me + hop, n_ctx)] < my_span
        k0, k1, v0, v1 = kbuf[hop, g, 0], kbuf[hop, g, 1], vbuf[hop, g, 0], vbuf[hop, g, 1]
        dv, dk, dq = unit(g, 1, k0, v0, False)
        dq_acc[g, 1] += dq
        picked = jnp.where(lower, 0, 1)
        dv_x, dk_x, dq_x = unit(
            g, picked, jnp.where(lower, k0, k1), jnp.where(lower, v0, v1), False
        )
        dq_acc[g, 0] += jnp.where(lower, dq_x, 0.0)
        dq_acc[g, 1] += jnp.where(lower, 0.0, dq_x)
        for which, first, second in ((0, dv, dv_x), (1, dk, dk_x)):
            early = first + jnp.where(lower, second, 0.0)
            late = jnp.where(lower, 0.0, second)
            if hop == WIN - 1:
                ret_send[g, hop - 1, which, 0] = early.astype(BF16)
                ret_send[g, hop - 1, which, 1] = late.astype(BF16)
                back(which, g, hop).start()
            else:
                part[g, hop - 1, which, 0] = early
                part[g, hop - 1, which, 1] = late

    def back(which, g, hop):
        return pltpu.make_async_remote_copy(
            src_ref=ret_send.at[g, hop - 1, which],
            dst_ref=ret_recv.at[g, hop - 1, which],
            send_sem=ret_ssem.at[which, g, hop - 1],
            recv_sem=ret_rsem.at[which, g, hop - 1],
            device_id=(right, my_head),
            device_id_type=MESH,
        )

    def pass_on(g, hop):
        for which in range(2):
            back(which, g, hop + 1).wait_recv()
            ret_send[g, hop - 1, which] = (
                ret_recv[g, hop, which].astype(F32) + part[g, hop - 1, which]
            ).astype(BF16)
            back(which, g, hop).start()

    stores = []

    def store(source, target):
        copy = pltpu.make_async_copy(source, target, store_sem.at[len(stores)])
        copy.start()
        stores.append(copy)

    def finish_query(g):
        for half in range(2):
            rows = slice(half * SPAN, (half + 1) * SPAN)
            cosine = tab_t[0, :, rows] * ROOT_SCALE
            sine = tab_t[1, :, rows] * ROOT_SCALE
            for j in range(share):
                stacked = slice(j * SPAN, (j + 1) * SPAN)
                first = dq_acc[g, half, 0:HALF, stacked]
                second = dq_acc[g, half, HALF:WIDTH, stacked]
                turned = jnp.concatenate(
                    [first * cosine + second * sine, second * cosine - first * sine], axis=0
                )
                head = g * share + j
                dq_out[rows, head * WIDTH : (head + 1) * WIDTH] = turned.T.astype(BF16)
        cols = slice(g * share * WIDTH, (g + 1) * share * WIDTH)
        store(dq_out.at[:, cols], dq_hbm.at[:, cols])

    def finish_keys(g):
        cols = slice(g * WIDTH, (g + 1) * WIDTH)
        for which, target in ((0, dv_hbm), (1, dk_hbm)):
            back(which, g, 1).wait_recv()
            for half in range(2):
                rows = slice(half * SPAN, (half + 1) * SPAN)
                total = own[g, which, half] + ret_recv[g, 0, which, half].astype(F32)
                if which == 1:
                    total = unrotated(total * ROOT_SCALE, half)
                dkv_out[which, rows, cols] = total.astype(BF16)
            store(dkv_out.at[which, :, cols], target.at[:, cols])

    got_v(0, 1)
    send_v(0, 2)
    for name in ("q", "g", "o", "lse"):
        loads[name].wait()
    prepare(0)
    got_k(0, 1)
    send_k(0, 2)
    got_v(0, 2)
    send_v(0, 3)
    own_block(0)
    got_k(0, 2)
    send_k(0, 3)
    send_k(1, 1)
    other_block(0, 1)
    got_v(1, 1)
    send_v(1, 2)
    other_block(0, 2)
    got_k(1, 1)
    send_k(1, 2)
    got_v(0, 3)
    got_k(0, 3)
    other_block(0, 3)
    prepare(1)
    got_v(1, 2)
    send_v(1, 3)
    pass_on(0, 2)
    own_block(1)
    got_k(1, 2)
    send_k(1, 3)
    pass_on(0, 1)
    other_block(1, 1)
    other_block(1, 2)
    got_v(1, 3)
    got_k(1, 3)
    other_block(1, 3)
    finish_query(0)
    finish_keys(0)
    pass_on(1, 2)
    finish_query(1)
    pass_on(1, 1)
    finish_keys(1)

    for copy in pos_copies:
        copy.wait_send()
    for g in range(groups):
        for which in range(2):
            for hop in range(1, WIN):
                forward(which, g, hop).wait_send()
                back(which, g, hop).wait_send()
    for copy in stores:
        copy.wait()


def shards(query, key, value, out_grad, attn_out, log_sum_exp, positions, span_map):
    rows = query.shape[0]
    heads = query.shape[1] // WIDTH
    groups = key.shape[1] // WIDTH
    share = heads // groups
    n_ctx = lax.axis_size("ctx")
    n_head = lax.axis_size("head")
    hops = WIN - 1
    dma = pltpu.SemaphoreType.DMA
    anywhere = pl.BlockSpec(memory_space=pl.ANY)
    return pl.pallas_call(
        functools.partial(kernel, groups, share, n_ctx, n_head),
        out_shape=(
            jax.ShapeDtypeStruct((rows, heads * WIDTH), BF16),
            jax.ShapeDtypeStruct((rows, groups * WIDTH), BF16),
            jax.ShapeDtypeStruct((rows, groups * WIDTH), BF16),
        ),
        in_specs=[pl.BlockSpec(memory_space=pltpu.SMEM)] + [anywhere] * 7,
        out_specs=(anywhere,) * 3,
        scratch_shapes=[
            pltpu.VMEM((rows, heads * WIDTH), BF16),
            pltpu.VMEM((rows, groups * WIDTH), BF16),
            pltpu.VMEM((rows, heads * WIDTH), BF16),
            pltpu.VMEM((rows, heads * WIDTH), BF16),
            pltpu.VMEM((heads, rows), F32),
            pltpu.VMEM((n_head,) + positions.shape, jnp.int32),
            pltpu.VMEM((groups, 2, share * SPAN, WIDTH), BF16),
            pltpu.VMEM((groups, 2, share * SPAN, WIDTH), BF16),
            pltpu.VMEM((groups, 2, 8, share * SPAN), F32),
            pltpu.VMEM((groups, 2, 8, share * SPAN), F32),
            pltpu.VMEM((2, HALF, rows), F32),
            pltpu.VMEM((2, rows, WIDTH), F32),
            pltpu.VMEM((WIN, groups, 2, SPAN, WIDTH), BF16),
            pltpu.VMEM((WIN, groups, 2, SPAN, WIDTH), BF16),
            pltpu.VMEM((groups, 2, WIDTH, share * SPAN), F32),
            pltpu.VMEM((rows, heads * WIDTH), BF16),
            pltpu.VMEM((groups, 2, 2, SPAN, WIDTH), F32),
            pltpu.VMEM((groups, hops - 1, 2, 2, SPAN, WIDTH), F32),
            pltpu.VMEM((groups, hops, 2, 2, SPAN, WIDTH), BF16),
            pltpu.VMEM((groups, hops, 2, 2, SPAN, WIDTH), BF16),
            pltpu.VMEM((2, rows, groups * WIDTH), BF16),
            dma((6 + 2 * groups,)),
            dma((3 * groups,)),
            dma((n_head - 1,)),
            dma((n_head - 1,)),
            dma((2, groups, hops)),
            dma((2, groups, hops)),
            dma((2, groups, hops)),
            dma((2, groups, hops)),
        ],
        compiler_params=pltpu.CompilerParams(
            collective_id=0, has_side_effects=True, vmem_limit_bytes=40 * 2**20
        ),
        cost_estimate=pl.CostEstimate(
            flops=10 * heads * 9 * SPAN * SPAN * WIDTH,
            bytes_accessed=8 * rows * heads * WIDTH + 8 * rows * groups * WIDTH,
            transcendentals=heads * 9 * SPAN * SPAN,
        ),
    )(span_map, query, key, value, out_grad, attn_out, log_sum_exp, positions)


def solution(mesh):
    placed = (
        P("ctx", "head"),
        P("ctx", "head"),
        P("ctx", "head"),
        P("ctx", "head"),
        P("ctx", "head"),
        P("head", "ctx"),
        P(None, ("ctx", "head")),
        P(),
    )
    return jax.shard_map(
        shards,
        mesh=mesh,
        in_specs=placed,
        out_specs=(P("ctx", "head"), P("ctx", "head"), P("ctx", "head")),
        check_vma=False,
    )
```

```python
import functools
import math

import jax
import jax.numpy as jnp
from jax import lax
from jax.experimental import pallas as pl
from jax.experimental.pallas import tpu as pltpu
from jax.sharding import PartitionSpec as P

WIDTH = 128
HALF = WIDTH // 2
SPAN = 128
WIN = 4
ROPE_BASE = 1000000.0
YARN_FACTOR = 4.0
YARN_INITIAL = 32768.0
BETA_FAST = 32.0
BETA_SLOW = 1.0
YARN_MSCALE = 1.0 + 0.1 * math.log(4.0)
ROOT_SCALE = 1.0 / math.sqrt(WIDTH)
LOG2E = math.log2(math.e)
F32 = jnp.float32
BF16 = jnp.bfloat16
MESH = pl.DeviceIdType.MESH
DIRECT = ()
ORDER = (
    ("prepare", 0),
    ("pass", 0, 1),
    ("pass", 2, 1),
    ("pass", 0, 2),
    ("pass", 1, 1),
    ("pass", 2, 2),
    ("pass", 3, 1),
    ("block", 0, 2),
    ("prepare", 1),
    ("block", 0, 3),
    ("pass", 1, 2),
    ("block", 2, 2),
    ("block", 2, 3),
    ("pass", 3, 2),
    ("return", 0, 2),
    ("block", 3, 1),
    ("block", 1, 3),
    ("block", 0, 1),
    ("return", 2, 2),
    ("block", 3, 3),
    ("return", 0, 1),
    ("block", 1, 2),
    ("block", 3, 2),
    ("return", 1, 2),
    ("block", 2, 1),
    ("own", 0),
    ("return", 3, 2),
    ("return", 2, 1),
    ("block", 1, 1),
    ("return", 1, 1),
    ("own", 1),
    ("return", 3, 1),
    ("keys", 0),
    ("query", 1),
    ("keys", 1),
    ("keys", 2),
    ("query", 0),
    ("keys", 3),
)


def half_pi_parts():
    a = math.floor(math.pi / 2 * 2**11) / 2**11
    rest = math.pi / 2 - a
    shift = 11 - math.floor(math.log2(rest))
    b = math.floor(rest * 2.0**shift) / 2.0**shift
    return a, b, rest - b


def cos_sin(angle):
    a, b, c = half_pi_parts()
    turns = jnp.floor(angle * (2.0 / math.pi) + 0.5)
    rest = ((angle - turns * a) - turns * b) - turns * c
    quadrant = turns.astype(jnp.int32) & 3
    square = rest * rest
    sine = rest + rest * square * (
        -1.0 / 6 + square * (1.0 / 120 + square * (-1.0 / 5040 + square * (1.0 / 362880)))
    )
    cosine = 1.0 + square * (
        -0.5
        + square
        * (1.0 / 24 + square * (-1.0 / 720 + square * (1.0 / 40320 - square * (1.0 / 3628800))))
    )
    swap = (quadrant & 1) == 1
    cos_out = jnp.where(swap, sine, cosine)
    sin_out = jnp.where(swap, cosine, sine)
    cos_out = jnp.where((quadrant == 1) | (quadrant == 2), -cos_out, cos_out)
    sin_out = jnp.where(quadrant >= 2, -sin_out, sin_out)
    return cos_out, sin_out


def frequencies(shape):
    pair = lax.broadcasted_iota(jnp.int32, shape, 0).astype(F32)
    inverse = jnp.exp(-2.0 * pair / WIDTH * math.log(ROPE_BASE))
    ratio = YARN_INITIAL * inverse / (2.0 * math.pi)
    ramp = jnp.clip((ratio - BETA_SLOW) / (BETA_FAST - BETA_SLOW), 0.0, 1.0)
    return inverse * ((1.0 - ramp) / YARN_FACTOR + ramp)


def dot(a, b, a_dim, b_dim):
    return lax.dot_general(a, b, (((a_dim,), (b_dim,)), ((), ())), preferred_element_type=F32)


def kernel(
    groups,
    share,
    n_ctx,
    n_head,
    span_ref,
    q_hbm,
    k_hbm,
    v_hbm,
    g_hbm,
    o_hbm,
    lse_hbm,
    pos_hbm,
    dq_hbm,
    dk_hbm,
    dv_hbm,
    q_raw,
    k_raw,
    g_raw,
    o_raw,
    lse_raw,
    pos_all,
    q_s,
    g_s,
    lse_s,
    delta_s,
    tab_t,
    tab_n,
    kv,
    dq_acc,
    dq_out,
    own,
    part,
    ret_send,
    ret_recv,
    dkv_out,
    load_sem,
    store_sem,
    pos_ssem,
    pos_rsem,
    fwd_ssem,
    fwd_rsem,
    ret_ssem,
    ret_rsem,
):
    me = lax.axis_index("ctx")
    my_head = lax.axis_index("head")
    left = lax.rem(me + (n_ctx - 1), n_ctx)
    right = lax.rem(me + 1, n_ctx)
    far = range(2, WIN) if DIRECT else ()
    peers = [lax.rem(my_head + step, n_head) for step in range(1, n_head)]

    loads = {}

    def load(name, index, source, target):
        loads[name] = pltpu.make_async_copy(source, target, load_sem.at[index])
        loads[name].start()

    load("pos", 0, pos_hbm, pos_all.at[my_head])
    chunks = 2 * groups
    for chunk in range(chunks):
        g, half = chunk // 2, chunk % 2
        load(
            ("v", chunk),
            1 + chunk,
            v_hbm.at[half * SPAN : (half + 1) * SPAN, g * WIDTH : (g + 1) * WIDTH],
            kv.at[0, chunk, 0],
        )
    base = 1 + chunks
    load("k", base, k_hbm, k_raw)
    load("q", base + 1, q_hbm, q_raw)
    load("g", base + 2, g_hbm, g_raw)
    load("o", base + 3, o_hbm, o_raw)
    load("lse", base + 4, lse_hbm, lse_raw)

    barrier = pltpu.get_barrier_semaphore()
    for ctx in [left, right] + [lax.rem(me + (n_ctx - hop), n_ctx) for hop in far]:
        pl.semaphore_signal(barrier, inc=1, device_id=(ctx, my_head), device_id_type=MESH)
    for peer in peers:
        pl.semaphore_signal(barrier, inc=1, device_id=(me, peer), device_id_type=MESH)
    freq = frequencies((HALF, WIDTH))
    loads["pos"].wait()
    pl.semaphore_wait(barrier, 2 + len(far) + len(peers))

    pos_copies = []
    for step, peer in enumerate(peers):
        copy = pltpu.make_async_remote_copy(
            src_ref=pos_all.at[my_head],
            dst_ref=pos_all.at[my_head],
            send_sem=pos_ssem.at[step],
            recv_sem=pos_rsem.at[step],
            device_id=(me, peer),
            device_id_type=MESH,
        )
        copy.start()
        pos_copies.append(copy)

    def forward(which, chunk, hop):
        return pltpu.make_async_remote_copy(
            src_ref=kv.at[hop - 1, chunk, which],
            dst_ref=kv.at[hop, chunk, which],
            send_sem=fwd_ssem.at[which, chunk, hop - 1],
            recv_sem=fwd_rsem.at[which, chunk, hop - 1],
            device_id=(left, my_head),
            device_id_type=MESH,
        )

    for chunk in range(chunks):
        loads[("v", chunk)].wait()
        forward(0, chunk, 1).start()

    for copy in pos_copies:
        copy.wait_recv()
    pieces = [pos_all[h].astype(F32) for h in range(n_head)]
    placed = jnp.concatenate(pieces, axis=1)
    pair = lax.broadcasted_iota(jnp.int32, (HALF, 2 * SPAN), 0)
    chosen = jnp.where(
        pair < WIDTH // 8,
        placed[0:1],
        jnp.where(pair < WIDTH // 8 + 3 * WIDTH // 16, placed[1:2], placed[2:3]),
    )
    cosine, sine = cos_sin(chosen * jnp.concatenate([freq, freq], axis=1))
    cosine = cosine * YARN_MSCALE
    sine = sine * YARN_MSCALE
    tab_t[0] = cosine
    tab_t[1] = sine
    tab_n[0] = jnp.concatenate([cosine, cosine], axis=0).T
    tab_n[1] = jnp.concatenate([-sine, sine], axis=0).T

    def rotated(block, half):
        wide = block.astype(F32)
        rows = slice(half * SPAN, (half + 1) * SPAN)
        return (wide * tab_n[0, rows] + pltpu.roll(wide, HALF, 1) * tab_n[1, rows]).astype(BF16)

    def unrotated(wide, half):
        rows = slice(half * SPAN, (half + 1) * SPAN)
        return wide * tab_n[0, rows] - pltpu.roll(wide, HALF, 1) * tab_n[1, rows]

    loads["k"].wait()
    for chunk in range(chunks):
        g, half = chunk // 2, chunk % 2
        kv[0, chunk, 1] = rotated(
            k_raw[half * SPAN : (half + 1) * SPAN, g * WIDTH : (g + 1) * WIDTH], half
        )
        forward(1, chunk, 1).start()

    def prepare(g):
        for half in range(2):
            rows = slice(half * SPAN, (half + 1) * SPAN)
            ones = jnp.ones((8, WIDTH), BF16)
            for j in range(share):
                head = g * share + j
                cols = slice(head * WIDTH, (head + 1) * WIDTH)
                stacked = slice(j * SPAN, (j + 1) * SPAN)
                q_s[g, half, stacked] = rotated(q_raw[rows, cols], half)
                grad = g_raw[rows, cols]
                g_s[g, half, stacked] = grad
                product = grad.astype(F32) * o_raw[rows, cols].astype(F32)
                upper = product.astype(BF16)
                lower = (product - upper.astype(F32)).astype(BF16)
                delta = dot(ones, upper, 1, 1) + dot(ones, lower, 1, 1)
                delta_s[g, half, :, stacked] = delta
                lse_s[g, half, :, stacked] = jnp.broadcast_to(
                    lse_raw[head : head + 1, rows] * LOG2E, (8, SPAN)
                )

    step_cols = 2 * SPAN

    def unit(g, q_half, key, value, causal=False, visible=None):
        value_sum = key_sum = None
        query_parts = []
        for start in range(0, share * SPAN, step_cols):
            at = slice(start, start + step_cols)
            query = q_s[g, q_half, at]
            grad = g_s[g, q_half, at]
            norm = lse_s[g, q_half, 0:1, at]
            if visible is not None:
                norm = jnp.where(visible, norm, 1e30)
            weights = jnp.exp2(dot(key, query, 1, 1) * (ROOT_SCALE * LOG2E) - norm)
            if causal:
                shape = (SPAN, step_cols)
                key_at = lax.broadcasted_iota(jnp.int32, shape, 0)
                query_at = lax.broadcasted_iota(jnp.int32, shape, 1) & (SPAN - 1)
                weights = jnp.where(key_at <= query_at, weights, 0.0)
            weight_grad = dot(value, grad, 1, 1)
            score_grad = weights * (weight_grad - delta_s[g, q_half, 0:1, at])
            rounded_weights = weights.astype(BF16)
            rounded_grad = score_grad.astype(BF16)
            value_part = dot(rounded_weights, grad, 1, 0)
            key_part = dot(rounded_grad, query, 1, 0)
            value_sum = value_part if value_sum is None else value_sum + value_part
            key_sum = key_part if key_sum is None else key_sum + key_part
            query_parts.append(dot(key, rounded_grad, 0, 0))
        return value_sum, key_sum, jnp.concatenate(query_parts, axis=1)

    my_span = span_ref[me]

    begun = set()

    def add_query(g, half, value):
        if (g, half) in begun:
            value = dq_acc[g, half] + value
        begun.add((g, half))
        dq_acc[g, half] = value

    def own_block(g):
        early, late = 2 * g, 2 * g + 1
        dv, dk, dq = unit(g, 0, kv[0, early, 1], kv[0, early, 0], causal=True)
        add_query(g, 0, dq)
        dv_next, dk_next, dq = unit(g, 1, kv[0, early, 1], kv[0, early, 0])
        own[early, 0] = dv + dv_next
        own[early, 1] = dk + dk_next
        dv, dk, dq_next = unit(g, 1, kv[0, late, 1], kv[0, late, 0], causal=True)
        own[late, 0] = dv
        own[late, 1] = dk
        add_query(g, 1, dq + dq_next)

    def got(chunk, hop):
        for which in range(2):
            forward(which, chunk, hop).wait_recv()

    def other_block(chunk, hop):
        g, half = chunk // 2, chunk % 2
        lower = span_ref[lax.rem(me + hop, n_ctx)] < my_span
        key, value = kv[hop, chunk, 1], kv[hop, chunk, 0]
        if half == 0:
            dv, dk, dq = unit(g, 1, key, value)
            add_query(g, 1, dq)
            dv_next, dk_next, dq = unit(g, 0, key, value, visible=lower)
            add_query(g, 0, dq)
            sums = (dv + dv_next, dk + dk_next)
        else:
            dv, dk, dq = unit(g, 1, key, value, visible=jnp.logical_not(lower))
            add_query(g, 1, dq)
            sums = (dv, dk)
        for which in range(2):
            if hop == WIN - 1 or chunk in DIRECT:
                ret_send[chunk, hop - 1, which] = sums[which].astype(BF16)
                back(which, chunk, hop).start()
            else:
                part[chunk, hop - 1, which] = sums[which]

    def back(which, chunk, hop):
        target = lax.rem(me + hop, n_ctx) if chunk in DIRECT else right
        return pltpu.make_async_remote_copy(
            src_ref=ret_send.at[chunk, hop - 1, which],
            dst_ref=ret_recv.at[chunk, hop - 1, which],
            send_sem=ret_ssem.at[which, chunk, hop - 1],
            recv_sem=ret_rsem.at[which, chunk, hop - 1],
            device_id=(target, my_head),
            device_id_type=MESH,
        )

    def pass_on(chunk, hop):
        for which in range(2):
            back(which, chunk, hop + 1).wait_recv()
            ret_send[chunk, hop - 1, which] = (
                ret_recv[chunk, hop, which].astype(F32) + part[chunk, hop - 1, which]
            ).astype(BF16)
            back(which, chunk, hop).start()

    stores = []

    def store(source, target):
        copy = pltpu.make_async_copy(source, target, store_sem.at[len(stores)])
        copy.start()
        stores.append(copy)

    def finish_query(g):
        for half in range(2):
            rows = slice(half * SPAN, (half + 1) * SPAN)
            cosine = tab_t[0, :, rows] * ROOT_SCALE
            sine = tab_t[1, :, rows] * ROOT_SCALE
            for j in range(share):
                stacked = slice(j * SPAN, (j + 1) * SPAN)
                first = dq_acc[g, half, 0:HALF, stacked]
                second = dq_acc[g, half, HALF:WIDTH, stacked]
                turned = jnp.concatenate(
                    [first * cosine + second * sine, second * cosine - first * sine], axis=0
                )
                head = g * share + j
                dq_out[rows, head * WIDTH : (head + 1) * WIDTH] = turned.T.astype(BF16)
        cols = slice(g * share * WIDTH, (g + 1) * share * WIDTH)
        store(dq_out.at[:, cols], dq_hbm.at[:, cols])

    def finish_keys(chunk):
        g, half = chunk // 2, chunk % 2
        rows = slice(half * SPAN, (half + 1) * SPAN)
        cols = slice(g * WIDTH, (g + 1) * WIDTH)
        for which, target in ((0, dv_hbm), (1, dk_hbm)):
            total = own[chunk, which]
            for hop in range(WIN - 1 if chunk in DIRECT else 1, 0, -1):
                back(which, chunk, hop).wait_recv()
                total = total + ret_recv[chunk, hop - 1, which].astype(F32)
            if which == 1:
                total = unrotated(total * ROOT_SCALE, half)
            dkv_out[which, rows, cols] = total.astype(BF16)
            store(dkv_out.at[which, rows, cols], target.at[rows, cols])

    for name in ("q", "g", "o", "lse"):
        loads[name].wait()
    for what, *at in ORDER:
        if what == "prepare":
            prepare(*at)
        elif what == "own":
            own_block(*at)
        elif what == "pass":
            chunk, hop = at
            got(chunk, hop)
            for which in range(2):
                forward(which, chunk, hop + 1).start()
        elif what == "block":
            chunk, hop = at
            if hop == WIN - 1:
                got(chunk, hop)
            other_block(chunk, hop)
        elif what == "return":
            pass_on(*at)
        elif what == "query":
            finish_query(*at)
        else:
            finish_keys(*at)

    for copy in pos_copies:
        copy.wait_send()
    for chunk in range(chunks):
        for which in range(2):
            for hop in range(1, WIN):
                forward(which, chunk, hop).wait_send()
                back(which, chunk, hop).wait_send()
    for copy in stores:
        copy.wait()


def shards(query, key, value, out_grad, attn_out, log_sum_exp, positions, span_map):
    rows = query.shape[0]
    heads = query.shape[1] // WIDTH
    groups = key.shape[1] // WIDTH
    share = heads // groups
    n_ctx = lax.axis_size("ctx")
    n_head = lax.axis_size("head")
    hops = WIN - 1
    chunks = 2 * groups
    dma = pltpu.SemaphoreType.DMA
    anywhere = pl.BlockSpec(memory_space=pl.ANY)
    return pl.pallas_call(
        functools.partial(kernel, groups, share, n_ctx, n_head),
        out_shape=(
            jax.ShapeDtypeStruct((rows, heads * WIDTH), BF16),
            jax.ShapeDtypeStruct((rows, groups * WIDTH), BF16),
            jax.ShapeDtypeStruct((rows, groups * WIDTH), BF16),
        ),
        in_specs=[pl.BlockSpec(memory_space=pltpu.SMEM)] + [anywhere] * 7,
        out_specs=(anywhere,) * 3,
        scratch_shapes=[
            pltpu.VMEM((rows, heads * WIDTH), BF16),
            pltpu.VMEM((rows, groups * WIDTH), BF16),
            pltpu.VMEM((rows, heads * WIDTH), BF16),
            pltpu.VMEM((rows, heads * WIDTH), BF16),
            pltpu.VMEM((heads, rows), F32),
            pltpu.VMEM((n_head,) + positions.shape, jnp.int32),
            pltpu.VMEM((groups, 2, share * SPAN, WIDTH), BF16),
            pltpu.VMEM((groups, 2, share * SPAN, WIDTH), BF16),
            pltpu.VMEM((groups, 2, 8, share * SPAN), F32),
            pltpu.VMEM((groups, 2, 8, share * SPAN), F32),
            pltpu.VMEM((2, HALF, rows), F32),
            pltpu.VMEM((2, rows, WIDTH), F32),
            pltpu.VMEM((WIN, chunks, 2, SPAN, WIDTH), BF16),
            pltpu.VMEM((groups, 2, WIDTH, share * SPAN), F32),
            pltpu.VMEM((rows, heads * WIDTH), BF16),
            pltpu.VMEM((chunks, 2, SPAN, WIDTH), F32),
            pltpu.VMEM((chunks, hops - 1, 2, SPAN, WIDTH), F32),
            pltpu.VMEM((chunks, hops, 2, SPAN, WIDTH), BF16),
            pltpu.VMEM((chunks, hops, 2, SPAN, WIDTH), BF16),
            pltpu.VMEM((2, rows, groups * WIDTH), BF16),
            dma((6 + chunks,)),
            dma((groups + 2 * chunks,)),
            dma((n_head - 1,)),
            dma((n_head - 1,)),
            dma((2, chunks, hops)),
            dma((2, chunks, hops)),
            dma((2, chunks, hops)),
            dma((2, chunks, hops)),
        ],
        compiler_params=pltpu.CompilerParams(
            collective_id=0, has_side_effects=True, vmem_limit_bytes=40 * 2**20
        ),
        cost_estimate=pl.CostEstimate(
            flops=10 * heads * 9 * SPAN * SPAN * WIDTH,
            bytes_accessed=8 * rows * heads * WIDTH + 8 * rows * groups * WIDTH,
            transcendentals=heads * 9 * SPAN * SPAN,
        ),
    )(
        *(
            pltpu.with_memory_space_constraint(x, pltpu.HBM)
            for x in (
                span_map, query, key, value, out_grad, attn_out, log_sum_exp, positions
            )
        ),
    )


def solution(mesh):
    placed = (
        P("ctx", "head"),
        P("ctx", "head"),
        P("ctx", "head"),
        P("ctx", "head"),
        P("ctx", "head"),
        P("head", "ctx"),
        P(None, ("ctx", "head")),
        P(),
    )
    return jax.shard_map(
        shards,
        mesh=mesh,
        in_specs=placed,
        out_specs=(P("ctx", "head"), P("ctx", "head"), P("ctx", "head")),
        check_vma=False,
    )
```

```python
import functools
import math

import jax
import jax.numpy as jnp
from jax import lax
from jax.experimental import pallas as pl
from jax.experimental.pallas import tpu as pltpu
from jax.sharding import PartitionSpec as P

WIDTH = 128
HALF = WIDTH // 2
SPAN = 128
WIN = 4
ROPE_BASE = 1000000.0
YARN_FACTOR = 4.0
YARN_INITIAL = 32768.0
BETA_FAST = 32.0
BETA_SLOW = 1.0
YARN_MSCALE = 1.0 + 0.1 * math.log(4.0)
ROOT_SCALE = 1.0 / math.sqrt(WIDTH)
LOG2E = math.log2(math.e)
F32 = jnp.float32
BF16 = jnp.bfloat16
MESH = pl.DeviceIdType.MESH
ORDER = (
    ("prepare", 1),
    ("prepare", 0),
    ("own", 0),
    ("pass", 0, 1),
    ("pass", 2, 1),
    ("pass", 1, 1),
    ("block", 2, 1),
    ("pass", 0, 2),
    ("block", 0, 2),
    ("pass", 3, 1),
    ("block", 3, 1),
    ("block", 0, 1),
    ("pass", 2, 2),
    ("block", 1, 2),
    ("block", 0, 3),
    ("block", 3, 2),
    ("block", 2, 3),
    ("block", 2, 2),
    ("return", 0, 2),
    ("block", 1, 1),
    ("return", 1, 1),
    ("return", 2, 2),
    ("return", 0, 1),
    ("own", 1),
    ("return", 3, 1),
    ("keys", 1),
    ("query", 1),
    ("query", 0),
    ("return", 2, 1),
    ("keys", 0),
    ("keys", 3),
    ("keys", 2),
)


def half_pi_parts():
    a = math.floor(math.pi / 2 * 2**11) / 2**11
    rest = math.pi / 2 - a
    shift = 11 - math.floor(math.log2(rest))
    b = math.floor(rest * 2.0**shift) / 2.0**shift
    return a, b, rest - b


def cos_sin(angle):
    a, b, c = half_pi_parts()
    turns = jnp.floor(angle * (2.0 / math.pi) + 0.5)
    rest = ((angle - turns * a) - turns * b) - turns * c
    quadrant = turns.astype(jnp.int32) & 3
    square = rest * rest
    sine = rest + rest * square * (
        -1.0 / 6 + square * (1.0 / 120 + square * (-1.0 / 5040 + square * (1.0 / 362880)))
    )
    cosine = 1.0 + square * (
        -0.5
        + square
        * (1.0 / 24 + square * (-1.0 / 720 + square * (1.0 / 40320 - square * (1.0 / 3628800))))
    )
    swap = (quadrant & 1) == 1
    cos_out = jnp.where(swap, sine, cosine)
    sin_out = jnp.where(swap, cosine, sine)
    cos_out = jnp.where((quadrant == 1) | (quadrant == 2), -cos_out, cos_out)
    sin_out = jnp.where(quadrant >= 2, -sin_out, sin_out)
    return cos_out, sin_out


def frequencies(shape):
    pair = lax.broadcasted_iota(jnp.int32, shape, 0).astype(F32)
    inverse = jnp.exp(-2.0 * pair / WIDTH * math.log(ROPE_BASE))
    ratio = YARN_INITIAL * inverse / (2.0 * math.pi)
    ramp = jnp.clip((ratio - BETA_SLOW) / (BETA_FAST - BETA_SLOW), 0.0, 1.0)
    return inverse * ((1.0 - ramp) / YARN_FACTOR + ramp)


def last_hop(chunk):
    return WIN - 1 - chunk % 2


def dot(a, b, a_dim, b_dim):
    return lax.dot_general(a, b, (((a_dim,), (b_dim,)), ((), ())), preferred_element_type=F32)


def kernel(
    groups,
    share,
    n_ctx,
    n_head,
    span_ref,
    q_hbm,
    k_hbm,
    v_hbm,
    g_hbm,
    o_hbm,
    lse_hbm,
    pos_hbm,
    dq_hbm,
    dk_hbm,
    dv_hbm,
    q_raw,
    k_raw,
    g_raw,
    o_raw,
    lse_raw,
    pos_all,
    q_s,
    g_s,
    stat_s,
    tab_t,
    tab_n,
    kv,
    far_q,
    far_g,
    far_stat,
    far_dq_send,
    far_dq_recv,
    dq_acc,
    dq_out,
    own,
    part,
    ret_send,
    ret_recv,
    dkv_out,
    load_sem,
    store_sem,
    pos_ssem,
    pos_rsem,
    fwd_ssem,
    fwd_rsem,
    ret_ssem,
    ret_rsem,
    far_ssem,
    far_rsem,
):
    me = lax.axis_index("ctx")
    my_head = lax.axis_index("head")
    left = lax.rem(me + (n_ctx - 1), n_ctx)
    right = lax.rem(me + 1, n_ctx)
    peers = [lax.rem(my_head + step, n_head) for step in range(1, n_head)]

    loads = {}

    def load(name, index, source, target):
        loads[name] = pltpu.make_async_copy(source, target, load_sem.at[index])
        loads[name].start()

    load("pos", 0, pos_hbm, pos_all.at[my_head])
    chunks = 2 * groups
    for chunk in range(chunks):
        g, half = chunk // 2, chunk % 2
        load(
            ("v", chunk),
            1 + chunk,
            v_hbm.at[half * SPAN : (half + 1) * SPAN, g * WIDTH : (g + 1) * WIDTH],
            kv.at[0, chunk, 0],
        )
    base = 1 + chunks
    load("k", base, k_hbm, k_raw)
    load("q", base + 1, q_hbm, q_raw)
    load("g", base + 2, g_hbm, g_raw)
    load("o", base + 3, o_hbm, o_raw)
    load("lse", base + 4, lse_hbm, lse_raw)

    barrier = pltpu.get_barrier_semaphore()
    for ctx in (left, right):
        pl.semaphore_signal(barrier, inc=1, device_id=(ctx, my_head), device_id_type=MESH)
    for peer in peers:
        pl.semaphore_signal(barrier, inc=1, device_id=(me, peer), device_id_type=MESH)
    freq = frequencies((HALF, WIDTH))
    for name in ("g", "o", "lse"):
        loads[name].wait()
    for g in range(groups):
        for half in range(2):
            rows = slice(half * SPAN, (half + 1) * SPAN)
            ones = jnp.ones((8, WIDTH), BF16)
            for j in range(share):
                head = g * share + j
                cols = slice(head * WIDTH, (head + 1) * WIDTH)
                stacked = slice(j * SPAN, (j + 1) * SPAN)
                grad = g_raw[rows, cols]
                g_s[g, half, stacked] = grad
                product = grad.astype(F32) * o_raw[rows, cols].astype(F32)
                upper = product.astype(BF16)
                lower = (product - upper.astype(F32)).astype(BF16)
                delta = dot(ones, upper, 1, 1) + dot(ones, lower, 1, 1)
                norm = lse_raw[head : head + 1, rows] * LOG2E
                first = lax.broadcasted_iota(jnp.int32, (8, SPAN), 0) == 0
                stat_s[g, half, :, stacked] = jnp.where(first, norm, delta)
    loads["pos"].wait()
    pl.semaphore_wait(barrier, 2 + len(peers))

    pos_copies = []
    for step, peer in enumerate(peers):
        copy = pltpu.make_async_remote_copy(
            src_ref=pos_all.at[my_head],
            dst_ref=pos_all.at[my_head],
            send_sem=pos_ssem.at[step],
            recv_sem=pos_rsem.at[step],
            device_id=(me, peer),
            device_id_type=MESH,
        )
        copy.start()
        pos_copies.append(copy)

    def forward(which, chunk, hop):
        return pltpu.make_async_remote_copy(
            src_ref=kv.at[hop - 1, chunk, which],
            dst_ref=kv.at[hop, chunk, which],
            send_sem=fwd_ssem.at[which, chunk, hop - 1],
            recv_sem=fwd_rsem.at[which, chunk, hop - 1],
            device_id=(left, my_head),
            device_id_type=MESH,
        )

    def move(g, what):
        source, target, place = (
            (q_s.at[g, 1], far_q.at[g], right),
            (g_s.at[g, 1], far_g.at[g], right),
            (stat_s.at[g, 1], far_stat.at[g], right),
            (far_dq_send.at[g], far_dq_recv.at[g], left),
        )[what]
        return pltpu.make_async_remote_copy(
            src_ref=source,
            dst_ref=target,
            send_sem=far_ssem.at[g, what],
            recv_sem=far_rsem.at[g, what],
            device_id=(place, my_head),
            device_id_type=MESH,
        )

    for chunk in range(chunks):
        loads[("v", chunk)].wait()
        forward(0, chunk, 1).start()
    for g in range(groups):
        move(g, 1).start()
        move(g, 2).start()

    for copy in pos_copies:
        copy.wait_recv()
    pieces = [pos_all[h].astype(F32) for h in range(n_head)]
    placed = jnp.concatenate(pieces, axis=1)
    pair = lax.broadcasted_iota(jnp.int32, (HALF, 2 * SPAN), 0)
    chosen = jnp.where(
        pair < WIDTH // 8,
        placed[0:1],
        jnp.where(pair < WIDTH // 8 + 3 * WIDTH // 16, placed[1:2], placed[2:3]),
    )
    cosine, sine = cos_sin(chosen * jnp.concatenate([freq, freq], axis=1))
    cosine = cosine * YARN_MSCALE
    sine = sine * YARN_MSCALE
    tab_t[0] = cosine
    tab_t[1] = sine
    tab_n[0] = jnp.concatenate([cosine, cosine], axis=0).T
    tab_n[1] = jnp.concatenate([-sine, sine], axis=0).T

    def rotated(block, half):
        wide = block.astype(F32)
        rows = slice(half * SPAN, (half + 1) * SPAN)
        return (wide * tab_n[0, rows] + pltpu.roll(wide, HALF, 1) * tab_n[1, rows]).astype(BF16)

    def unrotated(wide, half):
        rows = slice(half * SPAN, (half + 1) * SPAN)
        return wide * tab_n[0, rows] - pltpu.roll(wide, HALF, 1) * tab_n[1, rows]

    loads["k"].wait()
    for chunk in range(chunks):
        g, half = chunk // 2, chunk % 2
        kv[0, chunk, 1] = rotated(
            k_raw[half * SPAN : (half + 1) * SPAN, g * WIDTH : (g + 1) * WIDTH], half
        )
        forward(1, chunk, 1).start()

    def prepare(g):
        for half in (1, 0):
            rows = slice(half * SPAN, (half + 1) * SPAN)
            for j in range(share):
                head = g * share + j
                cols = slice(head * WIDTH, (head + 1) * WIDTH)
                q_s[g, half, j * SPAN : (j + 1) * SPAN] = rotated(q_raw[rows, cols], half)
            if half == 1:
                move(g, 0).start()

    step_cols = 2 * SPAN

    def unit(rows_of, key, value, causal=False, visible=None):
        q_rows, g_rows, stat = rows_of
        value_sum = key_sum = None
        query_parts = []
        for start in range(0, share * SPAN, step_cols):
            at = slice(start, start + step_cols)
            query = q_rows[at]
            grad = g_rows[at]
            norm = stat[0:1, at]
            if visible is not None:
                norm = jnp.where(visible, norm, 1e30)
            weights = jnp.exp2(dot(key, query, 1, 1) * (ROOT_SCALE * LOG2E) - norm)
            if causal:
                shape = (SPAN, step_cols)
                key_at = lax.broadcasted_iota(jnp.int32, shape, 0)
                query_at = lax.broadcasted_iota(jnp.int32, shape, 1) & (SPAN - 1)
                weights = jnp.where(key_at <= query_at, weights, 0.0)
            weight_grad = dot(value, grad, 1, 1)
            score_grad = weights * (weight_grad - stat[1:2, at])
            rounded_weights = weights.astype(BF16)
            rounded_grad = score_grad.astype(BF16)
            value_part = dot(rounded_weights, grad, 1, 0)
            key_part = dot(rounded_grad, query, 1, 0)
            value_sum = value_part if value_sum is None else value_sum + value_part
            key_sum = key_part if key_sum is None else key_sum + key_part
            query_parts.append(dot(key, rounded_grad, 0, 0))
        return value_sum, key_sum, jnp.concatenate(query_parts, axis=1)

    my_span = span_ref[me]

    def here(g, half):
        return q_s.at[g, half], g_s.at[g, half], stat_s.at[g, half]

    begun = set()

    def add_query(g, half, value):
        if (g, half) in begun:
            value = dq_acc[g, half] + value
        begun.add((g, half))
        dq_acc[g, half] = value

    def own_block(g):
        early, late = 2 * g, 2 * g + 1
        dv, dk, dq = unit(here(g, 0), kv[0, early, 1], kv[0, early, 0], causal=True)
        add_query(g, 0, dq)
        dv_next, dk_next, dq = unit(here(g, 1), kv[0, early, 1], kv[0, early, 0])
        own[early, 0] = dv + dv_next
        own[early, 1] = dk + dk_next
        dv, dk, dq_next = unit(here(g, 1), kv[0, late, 1], kv[0, late, 0], causal=True)
        own[late, 0] = dv
        own[late, 1] = dk
        add_query(g, 1, dq + dq_next)

    def got(chunk, hop):
        for which in range(2):
            forward(which, chunk, hop).wait_recv()

    def other_block(chunk, hop):
        g, half = chunk // 2, chunk % 2
        lower = span_ref[lax.rem(me + hop, n_ctx)] < my_span
        key, value = kv[hop, chunk, 1], kv[hop, chunk, 0]
        if half == 0:
            dv, dk, dq = unit(here(g, 1), key, value)
            add_query(g, 1, dq)
            dv_next, dk_next, dq = unit(here(g, 0), key, value, visible=lower)
            add_query(g, 0, dq)
            sums = (dv + dv_next, dk + dk_next)
        else:
            dv, dk, dq = unit(here(g, 1), key, value, visible=jnp.logical_not(lower))
            add_query(g, 1, dq)
            if hop == last_hop(chunk):
                for what in range(3):
                    move(g, what).wait_recv()
                far_visible = span_ref[lax.rem(me + hop, n_ctx)] > span_ref[left]
                dv_far, dk_far, dq_far = unit(
                    (far_q.at[g], far_g.at[g], far_stat.at[g]), key, value, visible=far_visible
                )
                dv = dv + dv_far
                dk = dk + dk_far
                far_dq_send[g] = dq_far.astype(BF16)
            sums = (dv, dk)
        for which in range(2):
            if hop == last_hop(chunk):
                ret_send[chunk, hop - 1, which] = sums[which].astype(BF16)
                back(which, chunk, hop).start()
            else:
                part[chunk, hop - 1, which] = sums[which]
        if half == 1 and hop == last_hop(chunk):
            move(g, 3).start()

    def back(which, chunk, hop):
        return pltpu.make_async_remote_copy(
            src_ref=ret_send.at[chunk, hop - 1, which],
            dst_ref=ret_recv.at[chunk, hop - 1, which],
            send_sem=ret_ssem.at[which, chunk, hop - 1],
            recv_sem=ret_rsem.at[which, chunk, hop - 1],
            device_id=(right, my_head),
            device_id_type=MESH,
        )

    def pass_on(chunk, hop):
        for which in range(2):
            back(which, chunk, hop + 1).wait_recv()
            ret_send[chunk, hop - 1, which] = (
                ret_recv[chunk, hop, which].astype(F32) + part[chunk, hop - 1, which]
            ).astype(BF16)
            back(which, chunk, hop).start()

    stores = []

    def store(source, target):
        copy = pltpu.make_async_copy(source, target, store_sem.at[len(stores)])
        copy.start()
        stores.append(copy)

    def finish_query(g):
        move(g, 3).wait_recv()
        for half in range(2):
            rows = slice(half * SPAN, (half + 1) * SPAN)
            cosine = tab_t[0, :, rows] * ROOT_SCALE
            sine = tab_t[1, :, rows] * ROOT_SCALE
            for j in range(share):
                stacked = slice(j * SPAN, (j + 1) * SPAN)
                first = dq_acc[g, half, 0:HALF, stacked]
                second = dq_acc[g, half, HALF:WIDTH, stacked]
                if half == 1:
                    first = first + far_dq_recv[g, 0:HALF, stacked].astype(F32)
                    second = second + far_dq_recv[g, HALF:WIDTH, stacked].astype(F32)
                turned = jnp.concatenate(
                    [first * cosine + second * sine, second * cosine - first * sine], axis=0
                )
                head = g * share + j
                dq_out[rows, head * WIDTH : (head + 1) * WIDTH] = turned.T.astype(BF16)
        cols = slice(g * share * WIDTH, (g + 1) * share * WIDTH)
        store(dq_out.at[:, cols], dq_hbm.at[:, cols])

    def finish_keys(chunk):
        g, half = chunk // 2, chunk % 2
        rows = slice(half * SPAN, (half + 1) * SPAN)
        cols = slice(g * WIDTH, (g + 1) * WIDTH)
        for which, target in ((0, dv_hbm), (1, dk_hbm)):
            back(which, chunk, 1).wait_recv()
            total = own[chunk, which] + ret_recv[chunk, 0, which].astype(F32)
            if which == 1:
                total = unrotated(total * ROOT_SCALE, half)
            dkv_out[which, rows, cols] = total.astype(BF16)
            store(dkv_out.at[which, rows, cols], target.at[rows, cols])

    loads["q"].wait()
    for what, *at in ORDER:
        if what == "prepare":
            prepare(*at)
        elif what == "own":
            own_block(*at)
        elif what == "pass":
            chunk, hop = at
            got(chunk, hop)
            for which in range(2):
                forward(which, chunk, hop + 1).start()
        elif what == "block":
            chunk, hop = at
            if hop == last_hop(chunk):
                got(chunk, hop)
            other_block(chunk, hop)
        elif what == "return":
            pass_on(*at)
        elif what == "query":
            finish_query(*at)
        else:
            finish_keys(*at)

    for copy in pos_copies:
        copy.wait_send()
    for chunk in range(chunks):
        for which in range(2):
            for hop in range(1, last_hop(chunk) + 1):
                forward(which, chunk, hop).wait_send()
                back(which, chunk, hop).wait_send()
    for g in range(groups):
        for what in range(4):
            move(g, what).wait_send()
    for copy in stores:
        copy.wait()


def shards(query, key, value, out_grad, attn_out, log_sum_exp, positions, span_map):
    rows = query.shape[0]
    heads = query.shape[1] // WIDTH
    groups = key.shape[1] // WIDTH
    share = heads // groups
    n_ctx = lax.axis_size("ctx")
    n_head = lax.axis_size("head")
    hops = WIN - 1
    chunks = 2 * groups
    dma = pltpu.SemaphoreType.DMA
    anywhere = pl.BlockSpec(memory_space=pl.ANY)
    return pl.pallas_call(
        functools.partial(kernel, groups, share, n_ctx, n_head),
        out_shape=(
            jax.ShapeDtypeStruct((rows, heads * WIDTH), BF16),
            jax.ShapeDtypeStruct((rows, groups * WIDTH), BF16),
            jax.ShapeDtypeStruct((rows, groups * WIDTH), BF16),
        ),
        in_specs=[pl.BlockSpec(memory_space=pltpu.SMEM)] + [anywhere] * 7,
        out_specs=(anywhere,) * 3,
        scratch_shapes=[
            pltpu.VMEM((rows, heads * WIDTH), BF16),
            pltpu.VMEM((rows, groups * WIDTH), BF16),
            pltpu.VMEM((rows, heads * WIDTH), BF16),
            pltpu.VMEM((rows, heads * WIDTH), BF16),
            pltpu.VMEM((heads, rows), F32),
            pltpu.VMEM((n_head,) + positions.shape, jnp.int32),
            pltpu.VMEM((groups, 2, share * SPAN, WIDTH), BF16),
            pltpu.VMEM((groups, 2, share * SPAN, WIDTH), BF16),
            pltpu.VMEM((groups, 2, 8, share * SPAN), F32),
            pltpu.VMEM((2, HALF, rows), F32),
            pltpu.VMEM((2, rows, WIDTH), F32),
            pltpu.VMEM((WIN, chunks, 2, SPAN, WIDTH), BF16),
            pltpu.VMEM((groups, share * SPAN, WIDTH), BF16),
            pltpu.VMEM((groups, share * SPAN, WIDTH), BF16),
            pltpu.VMEM((groups, 8, share * SPAN), F32),
            pltpu.VMEM((groups, WIDTH, share * SPAN), BF16),
            pltpu.VMEM((groups, WIDTH, share * SPAN), BF16),
            pltpu.VMEM((groups, 2, WIDTH, share * SPAN), F32),
            pltpu.VMEM((rows, heads * WIDTH), BF16),
            pltpu.VMEM((chunks, 2, SPAN, WIDTH), F32),
            pltpu.VMEM((chunks, hops - 1, 2, SPAN, WIDTH), F32),
            pltpu.VMEM((chunks, hops, 2, SPAN, WIDTH), BF16),
            pltpu.VMEM((chunks, hops, 2, SPAN, WIDTH), BF16),
            pltpu.VMEM((2, rows, groups * WIDTH), BF16),
            dma((6 + chunks,)),
            dma((groups + 2 * chunks,)),
            dma((n_head - 1,)),
            dma((n_head - 1,)),
            dma((2, chunks, hops)),
            dma((2, chunks, hops)),
            dma((2, chunks, hops)),
            dma((2, chunks, hops)),
            dma((groups, 4)),
            dma((groups, 4)),
        ],
        compiler_params=pltpu.CompilerParams(
            collective_id=0, has_side_effects=True, vmem_limit_bytes=40 * 2**20
        ),
        cost_estimate=pl.CostEstimate(
            flops=10 * heads * 9 * SPAN * SPAN * WIDTH,
            bytes_accessed=8 * rows * heads * WIDTH + 8 * rows * groups * WIDTH,
            transcendentals=heads * 9 * SPAN * SPAN,
        ),
    )(
        *(
            pltpu.with_memory_space_constraint(x, pltpu.HBM)
            for x in (
                span_map, query, key, value, out_grad, attn_out, log_sum_exp, positions
            )
        ),
    )


def solution(mesh):
    placed = (
        P("ctx", "head"),
        P("ctx", "head"),
        P("ctx", "head"),
        P("ctx", "head"),
        P("ctx", "head"),
        P("head", "ctx"),
        P(None, ("ctx", "head")),
        P(),
    )
    return jax.shard_map(
        shards,
        mesh=mesh,
        in_specs=placed,
        out_specs=(P("ctx", "head"), P("ctx", "head"), P("ctx", "head")),
        check_vma=False,
    )
```

```python
import functools
import math

import jax
import jax.numpy as jnp
from jax import lax
from jax.experimental import pallas as pl
from jax.experimental.pallas import tpu as pltpu
from jax.sharding import PartitionSpec as P

WIDTH = 128
HALF = WIDTH // 2
SPAN = 128
WIN = 4
ROPE_BASE = 1000000.0
YARN_FACTOR = 4.0
YARN_INITIAL = 32768.0
BETA_FAST = 32.0
BETA_SLOW = 1.0
YARN_MSCALE = 1.0 + 0.1 * math.log(4.0)
ROOT_SCALE = 1.0 / math.sqrt(WIDTH)
LOG2E = math.log2(math.e)
F32 = jnp.float32
BF16 = jnp.bfloat16
MESH = pl.DeviceIdType.MESH
ORDER = (
    ("prepare", 0),
    ("prepare", 1),
    ("own", 0),
    ("pass", 0, 1),
    ("pass", 2, 1),
    ("pass", 1, 1),
    ("own", 1),
    ("pass", 0, 2),
    ("block", 0, 2),
    ("pass", 2, 2),
    ("block", 2, 1),
    ("pass", 3, 1),
    ("block", 1, 2),
    ("block", 0, 3),
    ("block", 2, 3),
    ("block", 3, 2),
    ("block", 2, 2),
    ("return", 0, 2),
    ("block", 1, 1),
    ("block", 3, 1),
    ("return", 2, 2),
    ("block", 0, 1),
    ("return", 3, 1),
    ("return", 1, 1),
    ("return", 2, 1),
    ("return", 0, 1),
    ("query", 0),
    ("query", 1),
    ("keys", 2),
    ("keys", 1),
    ("keys", 3),
    ("keys", 0),
)


def half_pi_parts():
    a = math.floor(math.pi / 2 * 2**11) / 2**11
    rest = math.pi / 2 - a
    shift = 11 - math.floor(math.log2(rest))
    b = math.floor(rest * 2.0**shift) / 2.0**shift
    return a, b, rest - b


def cos_sin(angle):
    a, b, c = half_pi_parts()
    turns = jnp.floor(angle * (2.0 / math.pi) + 0.5)
    rest = ((angle - turns * a) - turns * b) - turns * c
    quadrant = turns.astype(jnp.int32) & 3
    square = rest * rest
    sine = rest + rest * square * (
        -1.0 / 6 + square * (1.0 / 120 + square * (-1.0 / 5040 + square * (1.0 / 362880)))
    )
    cosine = 1.0 + square * (
        -0.5
        + square
        * (1.0 / 24 + square * (-1.0 / 720 + square * (1.0 / 40320 - square * (1.0 / 3628800))))
    )
    swap = (quadrant & 1) == 1
    cos_out = jnp.where(swap, sine, cosine)
    sin_out = jnp.where(swap, cosine, sine)
    cos_out = jnp.where((quadrant == 1) | (quadrant == 2), -cos_out, cos_out)
    sin_out = jnp.where(quadrant >= 2, -sin_out, sin_out)
    return cos_out, sin_out


def frequencies(shape):
    pair = lax.broadcasted_iota(jnp.int32, shape, 0).astype(F32)
    inverse = jnp.exp(-2.0 * pair / WIDTH * math.log(ROPE_BASE))
    ratio = YARN_INITIAL * inverse / (2.0 * math.pi)
    ramp = jnp.clip((ratio - BETA_SLOW) / (BETA_FAST - BETA_SLOW), 0.0, 1.0)
    return inverse * ((1.0 - ramp) / YARN_FACTOR + ramp)


def last_hop(chunk):
    return WIN - 1 - chunk % 2


def dot(a, b, a_dim, b_dim):
    return lax.dot_general(a, b, (((a_dim,), (b_dim,)), ((), ())), preferred_element_type=F32)


def kernel(
    groups,
    share,
    n_ctx,
    n_head,
    span_ref,
    q_hbm,
    k_hbm,
    v_hbm,
    g_hbm,
    o_hbm,
    lse_hbm,
    pos_hbm,
    out_ref,
    q_raw,
    k_raw,
    g_raw,
    o_raw,
    lse_raw,
    pos_all,
    q_s,
    g_s,
    stat_s,
    tab_t,
    tab_n,
    kv,
    far_q,
    far_g,
    far_stat,
    far_dq_send,
    far_dq_recv,
    dq_acc,
    own,
    part,
    ret_send,
    ret_recv,
    load_sem,
    pos_ssem,
    pos_rsem,
    fwd_ssem,
    fwd_rsem,
    ret_ssem,
    ret_rsem,
    far_ssem,
    far_rsem,
):
    me = lax.axis_index("ctx")
    my_head = lax.axis_index("head")
    left = lax.rem(me + (n_ctx - 1), n_ctx)
    right = lax.rem(me + 1, n_ctx)
    peers = [lax.rem(my_head + step, n_head) for step in range(1, n_head)]

    barrier = pltpu.get_barrier_semaphore()
    for ctx in (left, right):
        pl.semaphore_signal(barrier, inc=1, device_id=(ctx, my_head), device_id_type=MESH)
    for peer in peers:
        pl.semaphore_signal(barrier, inc=1, device_id=(me, peer), device_id_type=MESH)
    loads = {}

    def load(name, index, source, target):
        loads[name] = pltpu.make_async_copy(source, target, load_sem.at[index])
        loads[name].start()

    load("pos", 0, pos_hbm, pos_all.at[my_head])
    chunks = 2 * groups
    for chunk in range(chunks):
        g, half = chunk // 2, chunk % 2
        load(
            ("v", chunk),
            1 + chunk,
            v_hbm.at[half * SPAN : (half + 1) * SPAN, g * WIDTH : (g + 1) * WIDTH],
            kv.at[0, chunk, 0],
        )
    base = 1 + chunks
    load("k", base, k_hbm, k_raw)
    load("q", base + 1, q_hbm, q_raw)
    load("g", base + 2, g_hbm, g_raw)
    load("o", base + 3, o_hbm, o_raw)
    load("lse", base + 4, lse_hbm, lse_raw)

    freq = frequencies((HALF, WIDTH))
    loads["pos"].wait()
    pl.semaphore_wait(barrier, 2 + len(peers))

    pos_copies = []
    for step, peer in enumerate(peers):
        copy = pltpu.make_async_remote_copy(
            src_ref=pos_all.at[my_head],
            dst_ref=pos_all.at[my_head],
            send_sem=pos_ssem.at[step],
            recv_sem=pos_rsem.at[step],
            device_id=(me, peer),
            device_id_type=MESH,
        )
        copy.start()
        pos_copies.append(copy)

    def forward(which, chunk, hop):
        return pltpu.make_async_remote_copy(
            src_ref=kv.at[hop - 1, chunk, which],
            dst_ref=kv.at[hop, chunk, which],
            send_sem=fwd_ssem.at[which, chunk, hop - 1],
            recv_sem=fwd_rsem.at[which, chunk, hop - 1],
            device_id=(left, my_head),
            device_id_type=MESH,
        )

    def move(g, what):
        source, target, place = (
            (q_s.at[g, 1], far_q.at[g], right),
            (g_s.at[g, 1], far_g.at[g], right),
            (stat_s.at[g, 1], far_stat.at[g], right),
            (far_dq_send.at[g], far_dq_recv.at[g], left),
        )[what]
        return pltpu.make_async_remote_copy(
            src_ref=source,
            dst_ref=target,
            send_sem=far_ssem.at[g, what],
            recv_sem=far_rsem.at[g, what],
            device_id=(place, my_head),
            device_id_type=MESH,
        )

    for chunk in range(chunks):
        loads[("v", chunk)].wait()
        forward(0, chunk, 1).start()

    for name in ("g", "o", "lse"):
        loads[name].wait()
    for g in range(groups):
        for half in range(2):
            rows = slice(half * SPAN, (half + 1) * SPAN)
            ones = jnp.ones((8, WIDTH), BF16)
            for j in range(share):
                head = g * share + j
                cols = slice(head * WIDTH, (head + 1) * WIDTH)
                stacked = slice(j * SPAN, (j + 1) * SPAN)
                grad = g_raw[rows, cols]
                g_s[g, half, stacked] = grad
                product = grad.astype(F32) * o_raw[rows, cols].astype(F32)
                upper = product.astype(BF16)
                lower = (product - upper.astype(F32)).astype(BF16)
                delta = dot(ones, upper, 1, 1) + dot(ones, lower, 1, 1)
                norm = lse_raw[head : head + 1, rows] * LOG2E
                first = lax.broadcasted_iota(jnp.int32, (8, SPAN), 0) == 0
                stat_s[g, half, :, stacked] = jnp.where(first, norm, delta)
        move(g, 1).start()
        move(g, 2).start()

    for copy in pos_copies:
        copy.wait_recv()
    pieces = [pos_all[h].astype(F32) for h in range(n_head)]
    placed = jnp.concatenate(pieces, axis=1)
    pair = lax.broadcasted_iota(jnp.int32, (HALF, 2 * SPAN), 0)
    chosen = jnp.where(
        pair < WIDTH // 8,
        placed[0:1],
        jnp.where(pair < WIDTH // 8 + 3 * WIDTH // 16, placed[1:2], placed[2:3]),
    )
    cosine, sine = cos_sin(chosen * jnp.concatenate([freq, freq], axis=1))
    cosine = cosine * YARN_MSCALE
    sine = sine * YARN_MSCALE
    tab_t[0] = cosine
    tab_t[1] = sine
    tab_n[0] = jnp.concatenate([cosine, cosine], axis=0).T
    tab_n[1] = jnp.concatenate([-sine, sine], axis=0).T

    def rotated(block, half):
        wide = block.astype(F32)
        rows = slice(half * SPAN, (half + 1) * SPAN)
        return (wide * tab_n[0, rows] + pltpu.roll(wide, HALF, 1) * tab_n[1, rows]).astype(BF16)

    def unrotated(wide, half):
        rows = slice(half * SPAN, (half + 1) * SPAN)
        return wide * tab_n[0, rows] - pltpu.roll(wide, HALF, 1) * tab_n[1, rows]

    loads["k"].wait()
    for chunk in range(chunks):
        g, half = chunk // 2, chunk % 2
        kv[0, chunk, 1] = rotated(
            k_raw[half * SPAN : (half + 1) * SPAN, g * WIDTH : (g + 1) * WIDTH], half
        )
        forward(1, chunk, 1).start()

    def prepare(g):
        for half in (1, 0):
            rows = slice(half * SPAN, (half + 1) * SPAN)
            for j in range(share):
                head = g * share + j
                cols = slice(head * WIDTH, (head + 1) * WIDTH)
                q_s[g, half, j * SPAN : (j + 1) * SPAN] = rotated(q_raw[rows, cols], half)
            if half == 1:
                move(g, 0).start()

    step_cols = 2 * SPAN

    def unit(rows_of, key, value, causal=False, visible=None):
        q_rows, g_rows, stat = rows_of
        value_sum = key_sum = None
        query_parts = []
        for start in range(0, share * SPAN, step_cols):
            at = slice(start, start + step_cols)
            query = q_rows[at]
            grad = g_rows[at]
            norm = stat[0:1, at]
            if visible is not None:
                norm = jnp.where(visible, norm, 1e30)
            weights = jnp.exp2(dot(key, query, 1, 1) * (ROOT_SCALE * LOG2E) - norm)
            if causal:
                shape = (SPAN, step_cols)
                key_at = lax.broadcasted_iota(jnp.int32, shape, 0)
                query_at = lax.broadcasted_iota(jnp.int32, shape, 1) & (SPAN - 1)
                weights = jnp.where(key_at <= query_at, weights, 0.0)
            weight_grad = dot(value, grad, 1, 1)
            score_grad = weights * (weight_grad - stat[1:2, at])
            rounded_weights = weights.astype(BF16)
            rounded_grad = score_grad.astype(BF16)
            value_part = dot(rounded_weights, grad, 1, 0)
            key_part = dot(rounded_grad, query, 1, 0)
            value_sum = value_part if value_sum is None else value_sum + value_part
            key_sum = key_part if key_sum is None else key_sum + key_part
            query_parts.append(dot(key, rounded_grad, 0, 0))
        return value_sum, key_sum, jnp.concatenate(query_parts, axis=1)

    my_span = span_ref[me]

    def here(g, half):
        return q_s.at[g, half], g_s.at[g, half], stat_s.at[g, half]

    begun = set()

    def add_query(g, half, value):
        if (g, half) in begun:
            value = dq_acc[g, half] + value
        begun.add((g, half))
        dq_acc[g, half] = value

    def own_block(g):
        early, late = 2 * g, 2 * g + 1
        dv, dk, dq = unit(here(g, 0), kv[0, early, 1], kv[0, early, 0], causal=True)
        add_query(g, 0, dq)
        dv_next, dk_next, dq = unit(here(g, 1), kv[0, early, 1], kv[0, early, 0])
        own[early, 0] = dv + dv_next
        own[early, 1] = dk + dk_next
        dv, dk, dq_next = unit(here(g, 1), kv[0, late, 1], kv[0, late, 0], causal=True)
        own[late, 0] = dv
        own[late, 1] = dk
        add_query(g, 1, dq + dq_next)

    def got(chunk, hop):
        for which in range(2):
            forward(which, chunk, hop).wait_recv()

    def other_block(chunk, hop):
        g, half = chunk // 2, chunk % 2
        lower = span_ref[lax.rem(me + hop, n_ctx)] < my_span
        key, value = kv[hop, chunk, 1], kv[hop, chunk, 0]
        if half == 0:
            dv, dk, dq = unit(here(g, 1), key, value)
            add_query(g, 1, dq)
            dv_next, dk_next, dq = unit(here(g, 0), key, value, visible=lower)
            add_query(g, 0, dq)
            sums = (dv + dv_next, dk + dk_next)
        else:
            dv, dk, dq = unit(here(g, 1), key, value, visible=jnp.logical_not(lower))
            add_query(g, 1, dq)
            if hop == last_hop(chunk):
                for what in range(3):
                    move(g, what).wait_recv()
                far_visible = span_ref[lax.rem(me + hop, n_ctx)] > span_ref[left]
                dv_far, dk_far, dq_far = unit(
                    (far_q.at[g], far_g.at[g], far_stat.at[g]), key, value, visible=far_visible
                )
                dv = dv + dv_far
                dk = dk + dk_far
                far_dq_send[g] = dq_far.astype(BF16)
            sums = (dv, dk)
        for which in range(2):
            if hop == last_hop(chunk):
                ret_send[chunk, hop - 1, which] = sums[which].astype(BF16)
                back(which, chunk, hop).start()
            else:
                part[chunk, hop - 1, which] = sums[which]
        if half == 1 and hop == last_hop(chunk):
            move(g, 3).start()

    def back(which, chunk, hop):
        return pltpu.make_async_remote_copy(
            src_ref=ret_send.at[chunk, hop - 1, which],
            dst_ref=ret_recv.at[chunk, hop - 1, which],
            send_sem=ret_ssem.at[which, chunk, hop - 1],
            recv_sem=ret_rsem.at[which, chunk, hop - 1],
            device_id=(right, my_head),
            device_id_type=MESH,
        )

    def pass_on(chunk, hop):
        for which in range(2):
            back(which, chunk, hop + 1).wait_recv()
            ret_send[chunk, hop - 1, which] = (
                ret_recv[chunk, hop, which].astype(F32) + part[chunk, hop - 1, which]
            ).astype(BF16)
            back(which, chunk, hop).start()

    def finish_query(g):
        move(g, 3).wait_recv()
        for half in range(2):
            rows = slice(half * SPAN, (half + 1) * SPAN)
            cosine = tab_t[0, :, rows] * ROOT_SCALE
            sine = tab_t[1, :, rows] * ROOT_SCALE
            for j in range(share):
                stacked = slice(j * SPAN, (j + 1) * SPAN)
                first = dq_acc[g, half, 0:HALF, stacked]
                second = dq_acc[g, half, HALF:WIDTH, stacked]
                if half == 1:
                    first = first + far_dq_recv[g, 0:HALF, stacked].astype(F32)
                    second = second + far_dq_recv[g, HALF:WIDTH, stacked].astype(F32)
                turned = jnp.concatenate(
                    [first * cosine + second * sine, second * cosine - first * sine], axis=0
                )
                head = g * share + j
                out_ref[rows, head * WIDTH : (head + 1) * WIDTH] = turned.T.astype(BF16)

    def finish_keys(chunk):
        g, half = chunk // 2, chunk % 2
        rows = slice(half * SPAN, (half + 1) * SPAN)
        for which in range(2):
            back(which, chunk, 1).wait_recv()
            total = own[chunk, which] + ret_recv[chunk, 0, which].astype(F32)
            if which == 1:
                total = unrotated(total * ROOT_SCALE, half)
            place = (groups * share + groups * (1 - which) + g) * WIDTH
            out_ref[rows, place : place + WIDTH] = total.astype(BF16)

    loads["q"].wait()
    for what, *at in ORDER:
        if what == "prepare":
            prepare(*at)
        elif what == "own":
            own_block(*at)
        elif what == "pass":
            chunk, hop = at
            got(chunk, hop)
            for which in range(2):
                forward(which, chunk, hop + 1).start()
        elif what == "block":
            chunk, hop = at
            if hop == last_hop(chunk):
                got(chunk, hop)
            other_block(chunk, hop)
        elif what == "return":
            pass_on(*at)
        elif what == "query":
            finish_query(*at)
        else:
            finish_keys(*at)

    for copy in pos_copies:
        copy.wait_send()
    for chunk in range(chunks):
        for which in range(2):
            for hop in range(1, last_hop(chunk) + 1):
                forward(which, chunk, hop).wait_send()
                back(which, chunk, hop).wait_send()
    for g in range(groups):
        for what in range(4):
            move(g, what).wait_send()


def shards(query, key, value, out_grad, attn_out, log_sum_exp, positions, span_map):
    rows = query.shape[0]
    heads = query.shape[1] // WIDTH
    groups = key.shape[1] // WIDTH
    share = heads // groups
    n_ctx = lax.axis_size("ctx")
    n_head = lax.axis_size("head")
    hops = WIN - 1
    chunks = 2 * groups
    dma = pltpu.SemaphoreType.DMA
    anywhere = pl.BlockSpec(memory_space=pl.ANY)
    merged = pl.pallas_call(
        functools.partial(kernel, groups, share, n_ctx, n_head),
        out_shape=jax.ShapeDtypeStruct((rows, (heads + 2 * groups) * WIDTH), BF16),
        in_specs=[pl.BlockSpec(memory_space=pltpu.SMEM)] + [anywhere] * 7,
        out_specs=pl.BlockSpec(memory_space=pltpu.VMEM),
        scratch_shapes=[
            pltpu.VMEM((rows, heads * WIDTH), BF16),
            pltpu.VMEM((rows, groups * WIDTH), BF16),
            pltpu.VMEM((rows, heads * WIDTH), BF16),
            pltpu.VMEM((rows, heads * WIDTH), BF16),
            pltpu.VMEM((heads, rows), F32),
            pltpu.VMEM((n_head,) + positions.shape, jnp.int32),
            pltpu.VMEM((groups, 2, share * SPAN, WIDTH), BF16),
            pltpu.VMEM((groups, 2, share * SPAN, WIDTH), BF16),
            pltpu.VMEM((groups, 2, 8, share * SPAN), F32),
            pltpu.VMEM((2, HALF, rows), F32),
            pltpu.VMEM((2, rows, WIDTH), F32),
            pltpu.VMEM((WIN, chunks, 2, SPAN, WIDTH), BF16),
            pltpu.VMEM((groups, share * SPAN, WIDTH), BF16),
            pltpu.VMEM((groups, share * SPAN, WIDTH), BF16),
            pltpu.VMEM((groups, 8, share * SPAN), F32),
            pltpu.VMEM((groups, WIDTH, share * SPAN), BF16),
            pltpu.VMEM((groups, WIDTH, share * SPAN), BF16),
            pltpu.VMEM((groups, 2, WIDTH, share * SPAN), F32),
            pltpu.VMEM((chunks, 2, SPAN, WIDTH), F32),
            pltpu.VMEM((chunks, hops - 1, 2, SPAN, WIDTH), F32),
            pltpu.VMEM((chunks, hops, 2, SPAN, WIDTH), BF16),
            pltpu.VMEM((chunks, hops, 2, SPAN, WIDTH), BF16),
            dma((6 + chunks,)),
            dma((n_head - 1,)),
            dma((n_head - 1,)),
            dma((2, chunks, hops)),
            dma((2, chunks, hops)),
            dma((2, chunks, hops)),
            dma((2, chunks, hops)),
            dma((groups, 4)),
            dma((groups, 4)),
        ],
        compiler_params=pltpu.CompilerParams(
            collective_id=0, has_side_effects=True, vmem_limit_bytes=40 * 2**20
        ),
        cost_estimate=pl.CostEstimate(
            flops=10 * heads * 9 * SPAN * SPAN * WIDTH,
            bytes_accessed=8 * rows * heads * WIDTH + 8 * rows * groups * WIDTH,
            transcendentals=heads * 9 * SPAN * SPAN,
        ),
    )(
        *(
            pltpu.with_memory_space_constraint(x, pltpu.HBM)
            for x in (
                span_map, query, key, value, out_grad, attn_out, log_sum_exp, positions
            )
        ),
    )
    first, second = heads * WIDTH, (heads + groups) * WIDTH
    return merged[:, :first], merged[:, first:second], merged[:, second:]


def solution(mesh):
    placed = (
        P("ctx", "head"),
        P("ctx", "head"),
        P("ctx", "head"),
        P("ctx", "head"),
        P("ctx", "head"),
        P("head", "ctx"),
        P(None, ("ctx", "head")),
        P(),
    )
    return jax.shard_map(
        shards,
        mesh=mesh,
        in_specs=placed,
        out_specs=(P("ctx", "head"), P("ctx", "head"), P("ctx", "head")),
        check_vma=False,
    )
```
